32 devices in a mesh: dist: 4 (over x, core), ctr: 8 (over z, y).
Axes of the slice: x: 2, y: 2, z: 4, core: 2. Of those that a mesh axis runs over, the one named last changes fastest.
Arguments:
- three_centre: bfloat16 [1024, 4, 4096], P(('dist', 'ctr')), may hold values from -0.359375 to 0.359375
- occupied_green: bfloat16 [128, 4096], P(('dist', 'ctr')), may hold values from -0.75 to 0.75
- virtual_green: bfloat16 [128, 4096], P(('dist', 'ctr')), may hold values from -0.75 to 0.75
- pair_index: int32 [16, 4], replicated, may hold values from 0 to 7, as said below
- source_slot: int32 [16, 4, 4], replicated, may hold values from -1 to 3, as said below
- occupied_index: int32 [16, 4, 4], replicated, may hold values from 0 to 127, as said below
- virtual_index: int32 [16, 4, 4], replicated, may hold values from 0 to 127, as said below
Outputs:
- density_response: float32 [1024, 256], P(('dist', 'ctr'))
The draws below stay inside these ranges and needn't reach their ends.
Inputs may be any that keep to these rules, and one draw needn't show every extreme that they name: `pair_index`: the 4 entries of a row are distinct. `source_slot`: for each slot the listed slots are distinct and come first, followed by -1 entries; all slots of one auxiliary atom list the same number of slots, at least 1; in every draw some auxiliary atom lists 4. `occupied_index`: for auxiliary atom p with g = p // 4, every entry lies in g * 32 to g * 32 + 2 * 32 - 1, taken modulo 128. `virtual_index`: for auxiliary atom p with g = p // 4, every entry lies in g * 32 to g * 32 + 2 * 32 - 1, taken modulo 128.
All inputs are finite; a program needn't handle non-finite values.
Results may differ from the reference program's by a relative error of at most 0.004.
Values may be sent and summed in bfloat16 or wider, within the bound.
A program may use at most 64 MiB of HBM per device.

```python
import jax
import jax.numpy as jnp
from jax import lax

BLK = 64
AUXB = 64
KP = 4
R = 4
PAIRW = 4096
NPR = 8
AUX = 1024
AUXA = 16
AUXR = 4
REGW = 256
NGB = 128
RGB = 32
N_DIST = 4


def draw_pair_index(key, part):
    keys = jax.random.split(jax.random.fold_in(key, 5), AUXA)
    rows = jax.vmap(lambda single: jax.random.permutation(single, NPR)[:KP])(keys)
    return rows.astype(jnp.int32)


def draw_source_slot(key, part):
    base = jax.random.fold_in(key, 11)
    first_key, count_key, full_key = jax.random.split(base, 3)
    keys = jax.random.split(first_key, AUXA * KP)
    picks = jax.vmap(lambda single: jax.random.permutation(single, KP)[:R])(keys).reshape(AUXA, KP, R)
    counts = jax.random.randint(count_key, (AUXA,), 1, R + 1)
    full_atom = jax.random.randint(full_key, (), 0, AUXA)
    counts = jnp.where(jnp.arange(AUXA) == full_atom, R, counts)
    live = jnp.arange(R)[None, None, :] < counts[:, None, None]
    return jnp.where(live, picks, -1).astype(jnp.int32)


def green_positions(key):
    region = jnp.arange(AUXA) // AUXR
    offset = jax.random.randint(key, (AUXA, KP, R), 0, 2 * RGB)
    return ((region[:, None, None] * RGB + offset) % NGB).astype(jnp.int32)


def draw_occupied_index(key, part):
    return green_positions(jax.random.fold_in(key, 21))


def draw_virtual_index(key, part):
    return green_positions(jax.random.fold_in(key, 22))


def block_levels(stream_key, extent, shards, least, high):
    gain = 1.0
    for axis_at, blocks in shards:
        steps = jax.random.uniform(jax.random.fold_in(jax.random.fold_in(stream_key, 6), axis_at), (blocks,), jnp.float32, least / len(shards), high / len(shards))
        gain = gain * jnp.repeat(jnp.exp(steps), extent[axis_at] // blocks).reshape((-1,) + (1,) * (len(extent) - 1 - axis_at))
    return gain


def noise(rng, extent, deviation, reach, cuts=(), held_as=jnp.bfloat16):
    entries = deviation * jax.random.normal(rng, extent, jnp.float32)
    if cuts:
        entries = entries * block_levels(rng, extent, cuts, -0.22, 0.18)
    return jnp.clip(entries, -reach, reach).astype(held_as)


def setup_inputs(seed: int = 0) -> dict:
    splits = jax.random.split(jax.random.key(seed), 8)
    three_centre = noise(splits[0], (AUX, KP, PAIRW), 0.06, 0.359375, ((0, 32),))
    occupied_green = noise(splits[1], (NGB, PAIRW), BLK ** -0.5, 0.75, ((0, 32),))
    virtual_green = noise(splits[2], (NGB, PAIRW), BLK ** -0.5, 0.75, ((0, 32),))
    pair_index = draw_pair_index(jax.random.fold_in(splits[7], 71), 0)
    source_slot = draw_source_slot(jax.random.fold_in(splits[7], 71), 0)
    occupied_index = draw_occupied_index(jax.random.fold_in(splits[7], 71), 0)
    virtual_index = draw_virtual_index(jax.random.fold_in(splits[7], 71), 0)
    return dict(three_centre=three_centre, occupied_green=occupied_green, virtual_green=virtual_green, pair_index=pair_index, source_slot=source_slot, occupied_index=occupied_index, virtual_index=virtual_index)


def green_apply(tensor_atom, source, occ_index, virt_index, occupied_green, virtual_green):
    accumulated = jnp.zeros(tensor_atom.shape, jnp.float32)
    occ_table = occupied_green.reshape(occupied_green.shape[0], BLK, BLK)
    virt_table = virtual_green.reshape(virtual_green.shape[0], BLK, BLK)
    for step in range(R):
        source_col = source[:, step]
        live_mask = (source_col >= 0).astype(jnp.float32)
        picked = jnp.take(tensor_atom, jnp.maximum(source_col, 0).astype(jnp.int32), axis=1)
        virt_blocks = jnp.take(virt_table, virt_index[:, step].astype(jnp.int32), axis=0)
        product = jnp.einsum('aslv,svz->aslz', picked.astype(jnp.float32), virt_blocks.astype(jnp.float32))
        product = (product * live_mask[None, :, None, None]).astype(jnp.bfloat16)
        product = lax.optimization_barrier(product)
        occ_blocks = jnp.take(occ_table, occ_index[:, step].astype(jnp.int32), axis=0)
        accumulated = accumulated + jnp.einsum('slm,aslz->asmz', occ_blocks.astype(jnp.float32), product.astype(jnp.float32))
    return accumulated.astype(jnp.bfloat16)


def region_response(inputs):
    upd_region, ten_region, pairs_region = inputs

    def row_atom(row_inputs):
        upd_atom, pairs_row = row_inputs

        def col_atom(col_inputs):
            ten_atom, pairs_col = col_inputs
            match = (pairs_row[:, None] == pairs_col[None, :]).astype(jnp.float32)
            matched = jnp.einsum('st,btc->sbc', match, ten_atom.astype(jnp.float32))
            return jnp.einsum('asc,sbc->ab', upd_atom.astype(jnp.float32), matched)

        blocks = lax.map(col_atom, (ten_region, pairs_region))
        return jnp.transpose(blocks, (1, 0, 2)).reshape(AUXB, REGW)

    row_blocks = lax.map(row_atom, (upd_region, pairs_region))
    return row_blocks.reshape(REGW, REGW)


def reference(three_centre, occupied_green, virtual_green, pair_index, source_slot, occupied_index, virtual_index):
    tensor_blocks = three_centre.reshape(AUXA, AUXB, KP, BLK, BLK)

    def one_atom(inputs):
        return green_apply(inputs[0], inputs[1], inputs[2], inputs[3], occupied_green, virtual_green)

    updated = lax.map(one_atom, (tensor_blocks, source_slot, occupied_index, virtual_index))
    updated = lax.optimization_barrier(updated)
    upd_regions = updated.reshape(N_DIST, AUXR, AUXB, KP, PAIRW)
    ten_regions = three_centre.reshape(N_DIST, AUXR, AUXB, KP, PAIRW)
    pair_regions = pair_index.reshape(N_DIST, AUXR, KP)
    result = lax.map(region_response, (upd_regions, ten_regions, pair_regions))
    return result.reshape(AUX, REGW)
```

```python
import functools

import jax
import jax.numpy as jnp
from jax import lax
from jax.experimental import pallas as pl
from jax.experimental.pallas import tpu as pltpu
from jax.sharding import PartitionSpec as P

BLK = 64
NPR = 8
LANES = 128
F32 = jnp.float32
BF16 = jnp.bfloat16


def kernel(n, groups, atoms, ids, t_ref, green_ref, out_ref, table, tf, tt, wcat, ocat, usend, urecv, trecv,
           uk, tk, part, precv, g_send, g_recv, t_send, t_recv, u_send, u_recv, p_send, p_recv, own_sem):
    slots, rows, width = t_ref.shape
    chunks = width // LANES
    blocks = green_ref.shape[0]
    cols = width // n
    per = cols // LANES
    dist = lax.axis_index("dist")
    me = lax.axis_index("ctr")
    before = lax.rem(dist + groups - 1, groups)
    after = lax.rem(dist + 1, groups)

    def ahead(k):
        return lax.rem(me + k, n)

    def signal(d, c):
        pl.semaphore_signal(barrier, inc=1, device_id=(d, c), device_id_type=pl.DeviceIdType.MESH)

    def remote(src, dst, send, recv, d, c):
        return pltpu.make_async_remote_copy(
            src_ref=src, dst_ref=dst, send_sem=send, recv_sem=recv, device_id=(d, c),
            device_id_type=pl.DeviceIdType.MESH,
        )

    barrier = pltpu.get_barrier_semaphore()
    for k in range(n):
        if k:
            signal(dist, ahead(k))
        signal(before, ahead(k))
        signal(after, ahead(k))

    row = lax.broadcasted_iota(jnp.int32, (BLK, BLK), 0)
    col = lax.broadcasted_iota(jnp.int32, (BLK, BLK), 1)
    half = BLK // 2
    wanted = jnp.where(row < half, 2 * row, 2 * (row - half) + 1)
    perm = (wanted == col).astype(BF16)
    mine = me * blocks
    for b in range(blocks):
        block = green_ref[b]
        occ = block[:, BLK:]
        turned = lax.dot_general(perm, occ, (((1,), (1,)), ((), ())), preferred_element_type=F32).astype(BF16)
        turned = lax.dot_general(turned, perm, (((1,), (1,)), ((), ())), preferred_element_type=F32).astype(BF16)
        table[mine + b] = jnp.concatenate([block[:, :BLK], turned], axis=1)

    pl.semaphore_wait(barrier, 3 * n - 1)

    green = []
    own = table.at[pl.ds(mine, blocks)]
    there = table.at[pl.ds(n * blocks + mine, blocks)]
    for k in range(n):
        if k:
            green.append(remote(own, own, g_send.at[0, k], g_recv.at[0, k], dist, ahead(k)))
        green.append(remote(own, there, g_send.at[1, k], g_recv.at[1, k], before, ahead(k)))
    for copy in green:
        copy.start()

    def t_part(c):
        return t_ref.at[:, :, pl.ds(pl.multiple_of(c * cols, LANES), cols)]

    tensor = [
        remote(t_part(ahead(k)), trecv.at[me], t_send.at[k], t_recv.at[k], dist, ahead(k)) for k in range(1, n)
    ]
    for copy in tensor:
        copy.start()
    own_t = pltpu.make_async_copy(t_part(me), trecv.at[me], own_sem.at[0])
    own_t.start()

    def turn(s, carry):
        for j in range(chunks):
            tf[j * rows:(j + 1) * rows, :] = t_ref[s, :, j * LANES:(j + 1) * LANES].astype(F32)
        for i in range(rows):
            tt[s, i * chunks:(i + 1) * chunks, :] = tf[pl.ds(i, chunks, stride=rows), :].astype(BF16)
        return carry

    lax.fori_loop(0, slots, turn, 0)

    for copy in green:
        copy.wait()

    size = atoms * slots
    atom = (dist * n + me) * rows // BLK
    total = n * blocks * groups
    base = dist * n * blocks

    def position(value):
        shift = value - base
        return jnp.minimum(jnp.where(shift < 0, shift + total, shift), 2 * n * blocks - 1)

    step_rows = 8 * chunks
    lane = lax.broadcasted_iota(jnp.int32, (half, LANES), 1)

    def update(s, carry):
        at = (atom * slots + s) * slots
        for r in range(slots):
            src = ids[at + r]
            live = jnp.where(src >= 0, 1.0, 0.0).astype(F32)
            src = jnp.maximum(src, 0)
            virt = table[position(ids[2 * size * slots + at + r])].astype(F32)[:, :BLK] * live
            zero = jnp.zeros((BLK, LANES), F32)
            twice = jnp.concatenate([virt, virt], axis=1)
            weight = jnp.concatenate(
                [jnp.concatenate([twice, zero], axis=1), jnp.concatenate([zero, twice], axis=1)], axis=0
            ).astype(BF16)
            ocat[:, r * BLK:(r + 1) * BLK] = table[position(ids[size * slots + at + r])][:, BLK:]
            for h in range(rows // 8):
                got = jnp.dot(
                    tt[src, h * step_rows:(h + 1) * step_rows, :], weight, preferred_element_type=F32
                ).astype(BF16)
                for x in range(8):
                    i = h * 8 + x
                    for e in range(2):
                        wcat[r * BLK + e * half:r * BLK + (e + 1) * half, i * LANES:(i + 1) * LANES] = got[
                            x * chunks:(x + 1) * chunks, e * LANES:(e + 1) * LANES
                        ]
        occ = ocat[...]
        for h in range(rows // 4):
            both = jnp.dot(occ, wcat[:, h * 4 * LANES:(h + 1) * 4 * LANES], preferred_element_type=F32)
            for x in range(4):
                i = h * 4 + x
                piece = both[:, x * LANES:(x + 1) * LANES]
                tf[i * chunks:(i + 1) * chunks, :] = jnp.where(lane < BLK, piece[:half], piece[half:])
        for q in range(chunks):
            usend[s, q // per, :, (q % per) * LANES:(q % per + 1) * LANES] = tf[
                pl.ds(q, rows, stride=chunks), :
            ].astype(BF16)
        for k in range(1, n):
            sent(s, k).start()
        return carry

    def sent(s, k):
        return remote(
            usend.at[s, ahead(k)], urecv.at[me, s], u_send.at[s, k], u_recv.at[s, k], dist, ahead(k)
        )

    lax.fori_loop(0, slots, update, 0)
    own_u = pltpu.make_async_copy(usend.at[:, me], urecv.at[me], own_sem.at[1])
    own_u.start()
    own_t.wait()
    own_u.wait()
    for copy in tensor:
        copy.wait()
    for s in range(slots):
        for k in range(1, n):
            sent(s, k).wait()

    part[...] = jnp.zeros_like(part)
    first = dist * (n * rows // BLK)
    pairs = 3 * size * slots

    def one_pair(pair, carry):
        def gather(p, inner):
            where = pairs + (first + p * rows // BLK) * slots
            slot = jnp.int32(0)
            live = jnp.int32(0)
            for s in range(slots):
                hit = ids[where + s] == pair
                slot = jnp.where(hit, s, slot)
                live = jnp.where(hit, 1, live)
            keep = live.astype(F32)
            at = pl.ds(pl.multiple_of(p * rows, rows), rows)
            uk[at, :] = (urecv[p, slot].astype(F32) * keep).astype(BF16)
            tk[at, :] = (trecv[p, slot].astype(F32) * keep).astype(BF16)
            return inner

        lax.fori_loop(0, n, gather, 0)

        def block(p, inner):
            at = pl.ds(pl.multiple_of(p * 256, 256), 256)
            part[at, :] += lax.dot_general(
                uk[at, :], tk[...], (((1,), (1,)), ((), ())), preferred_element_type=F32
            )
            return inner

        lax.fori_loop(0, n * rows // 256, block, 0)
        return carry

    lax.fori_loop(0, NPR, one_pair, 0)

    def p_part(c):
        return part.at[pl.ds(pl.multiple_of(c * rows, rows), rows)]

    shares = [
        remote(p_part(ahead(k)), precv.at[k], p_send.at[k], p_recv.at[k], dist, ahead(k)) for k in range(1, n)
    ]
    for copy in shares:
        copy.start()
    result = part[pl.ds(pl.multiple_of(me * rows, rows), rows), :]
    for k, copy in enumerate(shares, 1):
        copy.wait()
        result = result + precv[k]
    out_ref[...] = result


def solution(mesh):
    n = mesh.shape["ctr"]
    groups = mesh.shape["dist"]

    def shards(three_centre, occupied_green, virtual_green, pair_index, source_slot, occupied_index, virtual_index):
        rows, slots, width = three_centre.shape
        blocks = occupied_green.shape[0]
        atoms = pair_index.shape[0]
        chunks = width // LANES
        cols = width // n
        tensor = jnp.transpose(three_centre, (1, 0, 2))
        green = jnp.concatenate(
            [virtual_green.reshape(blocks, BLK, BLK), occupied_green.reshape(blocks, BLK, BLK)], axis=2
        )
        ids = jnp.concatenate(
            [x.reshape(-1) for x in (source_slot, occupied_index, virtual_index, pair_index)]
        )
        vmem = pl.BlockSpec(memory_space=pltpu.VMEM)
        dma = pltpu.SemaphoreType.DMA
        return pl.pallas_call(
            functools.partial(kernel, n, groups, atoms),
            out_shape=jax.ShapeDtypeStruct((rows, n * rows), F32),
            in_specs=[pl.BlockSpec(memory_space=pltpu.SMEM), vmem, vmem],
            out_specs=vmem,
            scratch_shapes=[
                pltpu.VMEM((2 * n * blocks, BLK, LANES), BF16),
                pltpu.VMEM((rows * chunks, LANES), F32),
                pltpu.VMEM((slots, rows * chunks, LANES), BF16),
                pltpu.VMEM((slots * BLK, rows * LANES), BF16),
                pltpu.VMEM((BLK, slots * BLK), BF16),
                pltpu.VMEM((slots, n, rows, cols), BF16),
                pltpu.VMEM((n, slots, rows, cols), BF16),
                pltpu.VMEM((n, slots, rows, cols), BF16),
                pltpu.VMEM((n * rows, cols), BF16),
                pltpu.VMEM((n * rows, cols), BF16),
                pltpu.VMEM((n * rows, n * rows), F32),
                pltpu.VMEM((n, rows, n * rows), F32),
                dma((2, n)),
                dma((2, n)),
                dma((n,)),
                dma((n,)),
                dma((slots, n)),
                dma((slots, n)),
                dma((n,)),
                dma((n,)),
                dma((2,)),
            ],
            compiler_params=pltpu.CompilerParams(
                collective_id=0, has_side_effects=True, vmem_limit_bytes=48 * 2**20
            ),
        )(ids, tensor, green)

    return jax.shard_map(
        shards,
        mesh=mesh,
        in_specs=(
            P(("dist", "ctr"), None, None),
            P(("dist", "ctr"), None),
            P(("dist", "ctr"), None),
            P(),
            P(),
            P(),
            P(),
        ),
        out_specs=P(("dist", "ctr"), None),
        check_vma=False,
    )
```

```python
import functools

import jax
import jax.numpy as jnp
from jax import lax
from jax.experimental import pallas as pl
from jax.experimental.pallas import tpu as pltpu
from jax.sharding import PartitionSpec as P

BLK = 64
NPR = 8
LANES = 128
F32 = jnp.float32
BF16 = jnp.bfloat16


def kernel(n, groups, atoms, ids, t_ref, green_ref, out_ref, table, tf, tt, wcat, ocat, usend, urecv, trecv,
           uk, tk, part, psend, precv, g_send, g_recv, t_send, t_recv, u_send, u_recv, p_send, p_recv, own_sem):
    slots, rows, width = t_ref.shape
    chunks = width // LANES
    blocks = green_ref.shape[0]
    cols = width // n
    per = cols // LANES
    dist = lax.axis_index("dist")
    me = lax.axis_index("ctr")
    before = lax.rem(dist + groups - 1, groups)
    after = lax.rem(dist + 1, groups)

    def ahead(k):
        return lax.rem(me + k, n)

    def signal(d, c):
        pl.semaphore_signal(barrier, inc=1, device_id=(d, c), device_id_type=pl.DeviceIdType.MESH)

    def remote(src, dst, send, recv, d, c):
        return pltpu.make_async_remote_copy(
            src_ref=src, dst_ref=dst, send_sem=send, recv_sem=recv, device_id=(d, c),
            device_id_type=pl.DeviceIdType.MESH,
        )

    barrier = pltpu.get_barrier_semaphore()
    for k in range(1, n):
        signal(dist, ahead(k))
    signal(before, me)
    signal(after, me)

    row = lax.broadcasted_iota(jnp.int32, (BLK, BLK), 0)
    col = lax.broadcasted_iota(jnp.int32, (BLK, BLK), 1)
    half = BLK // 2
    wanted = jnp.where(row < half, 2 * row, 2 * (row - half) + 1)
    perm = (wanted == col).astype(BF16)
    mine = me * blocks
    for b in range(blocks):
        block = green_ref[b]
        occ = block[:, BLK:]
        turned = lax.dot_general(perm, occ, (((1,), (1,)), ((), ())), preferred_element_type=F32).astype(BF16)
        turned = lax.dot_general(turned, perm, (((1,), (1,)), ((), ())), preferred_element_type=F32).astype(BF16)
        table[mine + b] = jnp.concatenate([block[:, :BLK], turned], axis=1)

    pl.semaphore_wait(barrier, n + 1)

    lines = n // 2
    high, low = me // 2, lax.rem(me, 2)
    partner = high * 2 + 1 - low

    def line(k):
        return lax.rem(high + k, lines) * 2

    def at_home(c):
        return table.at[pl.ds(c * blocks, blocks)]

    def across(c):
        return table.at[pl.ds((n + c) * blocks, blocks)]

    first_hop = [
        remote(at_home(me), at_home(me), g_send.at[0, k], g_recv.at[0, k], dist, line(k) + low)
        for k in range(1, lines)
    ]
    for copy in first_hop:
        copy.start()

    def t_part(c):
        return t_ref.at[:, :, pl.ds(pl.multiple_of(c * cols, LANES), cols)]

    tensor = [
        remote(t_part(ahead(k)), trecv.at[me], t_send.at[k], t_recv.at[k], dist, ahead(k)) for k in range(1, n)
    ]
    for copy in tensor:
        copy.start()
    own_t = pltpu.make_async_copy(t_part(me), trecv.at[me], own_sem.at[0])
    own_t.start()

    second_hop, third_hop = [], []
    for k in range(lines):
        if k:
            first_hop[k - 1].wait_recv()
        c = line(lines - k) + low
        second_hop.append(remote(at_home(c), at_home(c), g_send.at[1, k], g_recv.at[1, k], dist, partner))
        second_hop[-1].start()
        third_hop.append(remote(at_home(c), across(c), g_send.at[2, k], g_recv.at[2, k], before, me))
        third_hop[-1].start()

    def turn(s, carry):
        for j in range(chunks):
            tf[j * rows:(j + 1) * rows, :] = t_ref[s, :, j * LANES:(j + 1) * LANES].astype(F32)
        for i in range(rows):
            tt[s, i * chunks:(i + 1) * chunks, :] = tf[pl.ds(i, chunks, stride=rows), :].astype(BF16)
        return carry

    lax.fori_loop(0, slots, turn, 0)

    for k in range(lines):
        second_hop[k].wait_recv()
        c = line(lines - k) + 1 - low
        third_hop.append(remote(at_home(c), across(c), g_send.at[3, k], g_recv.at[3, k], before, me))
        third_hop[-1].start()
    for copy in third_hop:
        copy.wait()
    for copy in first_hop + second_hop:
        copy.wait_send()

    size = atoms * slots
    atom = (dist * n + me) * rows // BLK
    total = n * blocks * groups
    base = dist * n * blocks

    def position(value):
        shift = value - base
        return jnp.minimum(jnp.where(shift < 0, shift + total, shift), 2 * n * blocks - 1)

    step_rows = 8 * chunks
    lane = lax.broadcasted_iota(jnp.int32, (half, LANES), 1)

    def update(s, carry):
        at = (atom * slots + s) * slots
        for r in range(slots):
            src = ids[at + r]
            live = jnp.where(src >= 0, 1.0, 0.0).astype(F32)
            src = jnp.maximum(src, 0)
            virt = table[position(ids[2 * size * slots + at + r])].astype(F32)[:, :BLK] * live
            zero = jnp.zeros((BLK, LANES), F32)
            twice = jnp.concatenate([virt, virt], axis=1)
            weight = jnp.concatenate(
                [jnp.concatenate([twice, zero], axis=1), jnp.concatenate([zero, twice], axis=1)], axis=0
            ).astype(BF16)
            ocat[:, r * BLK:(r + 1) * BLK] = table[position(ids[size * slots + at + r])][:, BLK:]
            for h in range(rows // 8):
                got = jnp.dot(
                    tt[src, h * step_rows:(h + 1) * step_rows, :], weight, preferred_element_type=F32
                ).astype(BF16)
                for x in range(8):
                    i = h * 8 + x
                    for e in range(2):
                        wcat[r * BLK + e * half:r * BLK + (e + 1) * half, i * LANES:(i + 1) * LANES] = got[
                            x * chunks:(x + 1) * chunks, e * LANES:(e + 1) * LANES
                        ]
        occ = ocat[...]
        for h in range(rows // 4):
            both = jnp.dot(occ, wcat[:, h * 4 * LANES:(h + 1) * 4 * LANES], preferred_element_type=F32)
            for x in range(4):
                i = h * 4 + x
                piece = both[:, x * LANES:(x + 1) * LANES]
                tf[i * chunks:(i + 1) * chunks, :] = jnp.where(lane < BLK, piece[:half], piece[half:])
        for q in range(chunks):
            usend[s, q // per, :, (q % per) * LANES:(q % per + 1) * LANES] = tf[
                pl.ds(q, rows, stride=chunks), :
            ].astype(BF16)
        for k in range(1, n):
            sent(s, k).start()
        return carry

    def sent(s, k):
        return remote(
            usend.at[s, ahead(k)], urecv.at[me, s], u_send.at[s, k], u_recv.at[s, k], dist, ahead(k)
        )

    lax.fori_loop(0, slots, update, 0)
    own_u = pltpu.make_async_copy(usend.at[:, me], urecv.at[me], own_sem.at[1])
    own_u.start()
    own_t.wait()
    own_u.wait()
    for copy in tensor:
        copy.wait()
    for s in range(slots):
        for k in range(1, n):
            sent(s, k).wait()

    part[...] = jnp.zeros_like(part)
    first = dist * (n * rows // BLK)
    pairs = 3 * size * slots

    def one_pair(pair, carry):
        def gather(p, inner):
            where = pairs + (first + p * rows // BLK) * slots
            slot = jnp.int32(0)
            live = jnp.int32(0)
            for s in range(slots):
                hit = ids[where + s] == pair
                slot = jnp.where(hit, s, slot)
                live = jnp.where(hit, 1, live)
            keep = live.astype(F32)
            at = pl.ds(pl.multiple_of(p * rows, rows), rows)
            uk[at, :] = (urecv[p, slot].astype(F32) * keep).astype(BF16)
            tk[at, :] = (trecv[p, slot].astype(F32) * keep).astype(BF16)
            return inner

        lax.fori_loop(0, n, gather, 0)

        def block(p, inner):
            at = pl.ds(pl.multiple_of(p * 256, 256), 256)
            part[at, :] += lax.dot_general(
                uk[at, :], tk[...], (((1,), (1,)), ((), ())), preferred_element_type=F32
            )
            return inner

        lax.fori_loop(0, n * rows // 256, block, 0)
        return carry

    lax.fori_loop(0, NPR, one_pair, 0)

    psend[...] = part[...].astype(BF16)

    def p_part(c):
        return psend.at[pl.ds(pl.multiple_of(c * rows, rows), rows)]

    shares = [
        remote(p_part(ahead(k)), precv.at[k], p_send.at[k], p_recv.at[k], dist, ahead(k)) for k in range(1, n)
    ]
    for copy in shares:
        copy.start()
    result = part[pl.ds(pl.multiple_of(me * rows, rows), rows), :]
    for k, copy in enumerate(shares, 1):
        copy.wait()
        result = result + precv[k].astype(F32)
    out_ref[...] = result


def solution(mesh):
    n = mesh.shape["ctr"]
    groups = mesh.shape["dist"]

    def shards(three_centre, occupied_green, virtual_green, pair_index, source_slot, occupied_index, virtual_index):
        rows, slots, width = three_centre.shape
        blocks = occupied_green.shape[0]
        atoms = pair_index.shape[0]
        chunks = width // LANES
        cols = width // n
        tensor = jnp.transpose(three_centre, (1, 0, 2))
        green = jnp.concatenate(
            [virtual_green.reshape(blocks, BLK, BLK), occupied_green.reshape(blocks, BLK, BLK)], axis=2
        )
        ids = jnp.concatenate(
            [x.reshape(-1) for x in (source_slot, occupied_index, virtual_index, pair_index)]
        )
        vmem = pl.BlockSpec(memory_space=pltpu.VMEM)
        dma = pltpu.SemaphoreType.DMA
        return pl.pallas_call(
            functools.partial(kernel, n, groups, atoms),
            out_shape=jax.ShapeDtypeStruct((rows, n * rows), F32),
            in_specs=[pl.BlockSpec(memory_space=pltpu.SMEM), vmem, vmem],
            out_specs=vmem,
            scratch_shapes=[
                pltpu.VMEM((2 * n * blocks, BLK, LANES), BF16),
                pltpu.VMEM((rows * chunks, LANES), F32),
                pltpu.VMEM((slots, rows * chunks, LANES), BF16),
                pltpu.VMEM((slots * BLK, rows * LANES), BF16),
                pltpu.VMEM((BLK, slots * BLK), BF16),
                pltpu.VMEM((slots, n, rows, cols), BF16),
                pltpu.VMEM((n, slots, rows, cols), BF16),
                pltpu.VMEM((n, slots, rows, cols), BF16),
                pltpu.VMEM((n * rows, cols), BF16),
                pltpu.VMEM((n * rows, cols), BF16),
                pltpu.VMEM((n * rows, n * rows), F32),
                pltpu.VMEM((n * rows, n * rows), BF16),
                pltpu.VMEM((n, rows, n * rows), BF16),
                dma((4, n // 2)),
                dma((4, n // 2)),
                dma((n,)),
                dma((n,)),
                dma((slots, n)),
                dma((slots, n)),
                dma((n,)),
                dma((n,)),
                dma((2,)),
            ],
            compiler_params=pltpu.CompilerParams(
                collective_id=0, has_side_effects=True, vmem_limit_bytes=48 * 2**20
            ),
        )(ids, tensor, green)

    return jax.shard_map(
        shards,
        mesh=mesh,
        in_specs=(
            P(("dist", "ctr"), None, None),
            P(("dist", "ctr"), None),
            P(("dist", "ctr"), None),
            P(),
            P(),
            P(),
            P(),
        ),
        out_specs=P(("dist", "ctr"), None),
        check_vma=False,
    )
```

```python
import functools

import jax
import jax.numpy as jnp
from jax import lax
from jax.experimental import pallas as pl
from jax.experimental.pallas import tpu as pltpu
from jax.sharding import PartitionSpec as P

BLK = 64
NPR = 8
LANES = 128
F32 = jnp.float32
BF16 = jnp.bfloat16


def kernel(n, groups, atoms, ids, t_ref, green_ref, out_ref, table, tf, tt, wcat, ocat, usend, urecv, trecv,
           uk, tk, part, psend, precv, g_send, g_recv, t_send, t_recv, u_send, u_recv, p_send, p_recv, own_sem):
    slots, rows, width = t_ref.shape
    chunks = width // LANES
    blocks = green_ref.shape[0]
    team = n // 2
    cols = width // team
    per = cols // LANES
    dist = lax.axis_index("dist")
    me = lax.axis_index("ctr")
    before = lax.rem(dist + groups - 1, groups)
    after = lax.rem(dist + 1, groups)

    def ahead(k):
        return lax.rem(me + k, n)

    lead = me // team * team
    place = lax.rem(me, team)

    def mate(k):
        return lax.rem(place + k, team)

    def signal(d, c):
        pl.semaphore_signal(barrier, inc=1, device_id=(d, c), device_id_type=pl.DeviceIdType.MESH)

    def remote(src, dst, send, recv, d, c):
        return pltpu.make_async_remote_copy(
            src_ref=src, dst_ref=dst, send_sem=send, recv_sem=recv, device_id=(d, c),
            device_id_type=pl.DeviceIdType.MESH,
        )

    barrier = pltpu.get_barrier_semaphore()
    for k in range(1, n):
        signal(dist, ahead(k))
    signal(before, me)
    signal(after, me)

    row = lax.broadcasted_iota(jnp.int32, (BLK, BLK), 0)
    col = lax.broadcasted_iota(jnp.int32, (BLK, BLK), 1)
    half = BLK // 2
    wanted = jnp.where(row < half, 2 * row, 2 * (row - half) + 1)
    perm = (wanted == col).astype(BF16)
    mine = me * blocks
    for b in range(blocks):
        block = green_ref[b]
        occ = block[:, BLK:]
        turned = lax.dot_general(perm, occ, (((1,), (1,)), ((), ())), preferred_element_type=F32).astype(BF16)
        turned = lax.dot_general(turned, perm, (((1,), (1,)), ((), ())), preferred_element_type=F32).astype(BF16)
        table[mine + b] = jnp.concatenate([block[:, :BLK], turned], axis=1)

    pl.semaphore_wait(barrier, n + 1)

    lines = n // 2
    high, low = me // 2, lax.rem(me, 2)
    partner = high * 2 + 1 - low

    def line(k):
        return lax.rem(high + k, lines) * 2

    def at_home(c):
        return table.at[pl.ds(c * blocks, blocks)]

    def across(c):
        return table.at[pl.ds((n + c) * blocks, blocks)]

    first_hop = [
        remote(at_home(me), at_home(me), g_send.at[0, k], g_recv.at[0, k], dist, line(k) + low)
        for k in range(1, lines)
    ]
    for copy in first_hop:
        copy.start()

    def t_part(c):
        return t_ref.at[:, :, pl.ds(pl.multiple_of(lax.rem(c, team) * cols, LANES), cols)]

    tensor = [
        remote(t_part(ahead(k)), trecv.at[me], t_send.at[k], t_recv.at[k], dist, ahead(k)) for k in range(1, n)
    ]
    for copy in tensor:
        copy.start()
    own_t = pltpu.make_async_copy(t_part(me), trecv.at[me], own_sem.at[0])
    own_t.start()

    second_hop, third_hop = [], []
    for k in range(lines):
        if k:
            first_hop[k - 1].wait_recv()
        c = line(lines - k) + low
        second_hop.append(remote(at_home(c), at_home(c), g_send.at[1, k], g_recv.at[1, k], dist, partner))
        second_hop[-1].start()
        third_hop.append(remote(at_home(c), across(c), g_send.at[2, k], g_recv.at[2, k], before, me))
        third_hop[-1].start()

    def turn(s, carry):
        for j in range(chunks):
            tf[j * rows:(j + 1) * rows, :] = t_ref[s, :, j * LANES:(j + 1) * LANES].astype(F32)
        for i in range(rows):
            tt[s, i * chunks:(i + 1) * chunks, :] = tf[pl.ds(i, chunks, stride=rows), :].astype(BF16)
        return carry

    lax.fori_loop(0, slots, turn, 0)

    for k in range(lines):
        second_hop[k].wait_recv()
        c = line(lines - k) + 1 - low
        third_hop.append(remote(at_home(c), across(c), g_send.at[3, k], g_recv.at[3, k], before, me))
        third_hop[-1].start()
    for copy in third_hop:
        copy.wait()
    for copy in first_hop + second_hop:
        copy.wait_send()

    size = atoms * slots
    atom = (dist * n + me) * rows // BLK
    total = n * blocks * groups
    base = dist * n * blocks

    def position(value):
        shift = value - base
        return jnp.minimum(jnp.where(shift < 0, shift + total, shift), 2 * n * blocks - 1)

    step_rows = 8 * chunks
    lane = lax.broadcasted_iota(jnp.int32, (half, LANES), 1)

    def update(s, carry):
        at = (atom * slots + s) * slots
        for r in range(slots):
            src = ids[at + r]
            live = jnp.where(src >= 0, 1.0, 0.0).astype(F32)
            src = jnp.maximum(src, 0)
            virt = table[position(ids[2 * size * slots + at + r])].astype(F32)[:, :BLK] * live
            zero = jnp.zeros((BLK, LANES), F32)
            twice = jnp.concatenate([virt, virt], axis=1)
            weight = jnp.concatenate(
                [jnp.concatenate([twice, zero], axis=1), jnp.concatenate([zero, twice], axis=1)], axis=0
            ).astype(BF16)
            ocat[:, r * BLK:(r + 1) * BLK] = table[position(ids[size * slots + at + r])][:, BLK:]
            for h in range(rows // 8):
                got = jnp.dot(
                    tt[src, h * step_rows:(h + 1) * step_rows, :], weight, preferred_element_type=F32
                ).astype(BF16)
                for x in range(8):
                    i = h * 8 + x
                    for e in range(2):
                        wcat[r * BLK + e * half:r * BLK + (e + 1) * half, i * LANES:(i + 1) * LANES] = got[
                            x * chunks:(x + 1) * chunks, e * LANES:(e + 1) * LANES
                        ]
        occ = ocat[...]
        for h in range(rows // 4):
            both = jnp.dot(occ, wcat[:, h * 4 * LANES:(h + 1) * 4 * LANES], preferred_element_type=F32)
            for x in range(4):
                i = h * 4 + x
                piece = both[:, x * LANES:(x + 1) * LANES]
                tf[i * chunks:(i + 1) * chunks, :] = jnp.where(lane < BLK, piece[:half], piece[half:])
        for q in range(chunks):
            usend[s, q // per, :, (q % per) * LANES:(q % per + 1) * LANES] = tf[
                pl.ds(q, rows, stride=chunks), :
            ].astype(BF16)
        for k in range(1, team):
            sent(s, k).start()
        return carry

    def sent(s, k):
        return remote(
            usend.at[s, mate(k)], urecv.at[place, s], u_send.at[s, k], u_recv.at[s, k], dist, lead + mate(k)
        )

    lax.fori_loop(0, slots, update, 0)
    own_u = pltpu.make_async_copy(usend.at[:, place], urecv.at[place], own_sem.at[1])
    own_u.start()
    own_t.wait()
    own_u.wait()
    for copy in tensor:
        copy.wait()
    for s in range(slots):
        for k in range(1, team):
            sent(s, k).wait()

    part[...] = jnp.zeros_like(part)
    first = dist * (n * rows // BLK)
    pairs = 3 * size * slots

    def one_pair(pair, carry):
        def pick(dst, src, owner, p):
            where = pairs + (first + owner * rows // BLK) * slots
            slot = jnp.int32(0)
            live = jnp.int32(0)
            for s in range(slots):
                hit = ids[where + s] == pair
                slot = jnp.where(hit, s, slot)
                live = jnp.where(hit, 1, live)
            at = pl.ds(pl.multiple_of(p * rows, rows), rows)
            dst[at, :] = (src[p, slot].astype(F32) * live.astype(F32)).astype(BF16)

        def gather_t(p, inner):
            pick(tk, trecv, p, p)
            return inner

        def gather_u(p, inner):
            pick(uk, urecv, lead + p, p)
            return inner

        lax.fori_loop(0, n, gather_t, 0)
        lax.fori_loop(0, team, gather_u, 0)

        def block(p, inner):
            at = pl.ds(pl.multiple_of(p * LANES, LANES), LANES)
            part[at, :] += lax.dot_general(
                uk[at, :], tk[...], (((1,), (1,)), ((), ())), preferred_element_type=F32
            )
            return inner

        lax.fori_loop(0, team * rows // LANES, block, 0)
        return carry

    lax.fori_loop(0, NPR, one_pair, 0)

    psend[...] = part[...].astype(BF16)

    def p_part(c):
        return psend.at[pl.ds(pl.multiple_of(c * rows, rows), rows)]

    shares = [
        remote(p_part(mate(k)), precv.at[k], p_send.at[k], p_recv.at[k], dist, lead + mate(k))
        for k in range(1, team)
    ]
    for copy in shares:
        copy.start()
    result = part[pl.ds(pl.multiple_of(place * rows, rows), rows), :]
    for k, copy in enumerate(shares, 1):
        copy.wait()
        result = result + precv[k].astype(F32)
    out_ref[...] = result


def solution(mesh):
    n = mesh.shape["ctr"]
    groups = mesh.shape["dist"]

    def shards(three_centre, occupied_green, virtual_green, pair_index, source_slot, occupied_index, virtual_index):
        rows, slots, width = three_centre.shape
        blocks = occupied_green.shape[0]
        atoms = pair_index.shape[0]
        chunks = width // LANES
        team = n // 2
        cols = width // team
        tensor = jnp.transpose(three_centre, (1, 0, 2))
        green = jnp.concatenate(
            [virtual_green.reshape(blocks, BLK, BLK), occupied_green.reshape(blocks, BLK, BLK)], axis=2
        )
        ids = jnp.concatenate(
            [x.reshape(-1) for x in (source_slot, occupied_index, virtual_index, pair_index)]
        )
        vmem = pl.BlockSpec(memory_space=pltpu.VMEM)
        dma = pltpu.SemaphoreType.DMA
        return pl.pallas_call(
            functools.partial(kernel, n, groups, atoms),
            out_shape=jax.ShapeDtypeStruct((rows, n * rows), F32),
            in_specs=[pl.BlockSpec(memory_space=pltpu.SMEM), vmem, vmem],
            out_specs=vmem,
            scratch_shapes=[
                pltpu.VMEM((2 * n * blocks, BLK, LANES), BF16),
                pltpu.VMEM((rows * chunks, LANES), F32),
                pltpu.VMEM((slots, rows * chunks, LANES), BF16),
                pltpu.VMEM((slots * BLK, rows * LANES), BF16),
                pltpu.VMEM((BLK, slots * BLK), BF16),
                pltpu.VMEM((slots, team, rows, cols), BF16),
                pltpu.VMEM((team, slots, rows, cols), BF16),
                pltpu.VMEM((n, slots, rows, cols), BF16),
                pltpu.VMEM((team * rows, cols), BF16),
                pltpu.VMEM((n * rows, cols), BF16),
                pltpu.VMEM((team * rows, n * rows), F32),
                pltpu.VMEM((team * rows, n * rows), BF16),
                pltpu.VMEM((team, rows, n * rows), BF16),
                dma((4, n // 2)),
                dma((4, n // 2)),
                dma((n,)),
                dma((n,)),
                dma((slots, team)),
                dma((slots, team)),
                dma((team,)),
                dma((team,)),
                dma((2,)),
            ],
            compiler_params=pltpu.CompilerParams(
                collective_id=0, has_side_effects=True, vmem_limit_bytes=48 * 2**20
            ),
        )(ids, tensor, green)

    return jax.shard_map(
        shards,
        mesh=mesh,
        in_specs=(
            P(("dist", "ctr"), None, None),
            P(("dist", "ctr"), None),
            P(("dist", "ctr"), None),
            P(),
            P(),
            P(),
            P(),
        ),
        out_specs=P(("dist", "ctr"), None),
        check_vma=False,
    )
```

```python
import functools

import jax
import jax.numpy as jnp
from jax import lax
from jax.experimental import pallas as pl
from jax.experimental.pallas import tpu as pltpu
from jax.sharding import PartitionSpec as P

BLK = 64
NPR = 8
LANES = 128
F32 = jnp.float32
BF16 = jnp.bfloat16


def kernel(n, groups, atoms, ids, t_ref, green_ref, out_ref, table, tf, tt, wcat, ocat, usend, urecv, trecv,
           uk, tk, part, psend, precv, g_send, g_recv, t_send, t_recv, u_send, u_recv, p_send, p_recv, own_sem):
    slots, rows, width = t_ref.shape
    chunks = width // LANES
    blocks = green_ref.shape[0]
    cols = width // n
    per = cols // LANES
    dist = lax.axis_index("dist")
    me = lax.axis_index("ctr")
    before = lax.rem(dist + groups - 1, groups)
    after = lax.rem(dist + 1, groups)

    far_first = sorted(range(1, n), key=lambda k: -min(k, n - k))

    def ahead(k):
        return lax.rem(me + k, n)

    def signal(d, c):
        pl.semaphore_signal(barrier, inc=1, device_id=(d, c), device_id_type=pl.DeviceIdType.MESH)

    def remote(src, dst, send, recv, d, c):
        return pltpu.make_async_remote_copy(
            src_ref=src, dst_ref=dst, send_sem=send, recv_sem=recv, device_id=(d, c),
            device_id_type=pl.DeviceIdType.MESH,
        )

    barrier = pltpu.get_barrier_semaphore()
    for k in range(1, n):
        signal(dist, ahead(k))
    signal(before, me)
    signal(after, me)

    row = lax.broadcasted_iota(jnp.int32, (BLK, BLK), 0)
    col = lax.broadcasted_iota(jnp.int32, (BLK, BLK), 1)
    half = BLK // 2
    wanted = jnp.where(row < half, 2 * row, 2 * (row - half) + 1)
    perm = (wanted == col).astype(BF16)
    mine = me * blocks
    for b in range(blocks):
        block = green_ref[b]
        occ = block[:, BLK:]
        turned = lax.dot_general(perm, occ, (((1,), (1,)), ((), ())), preferred_element_type=F32).astype(BF16)
        turned = lax.dot_general(turned, perm, (((1,), (1,)), ((), ())), preferred_element_type=F32).astype(BF16)
        table[mine + b] = jnp.concatenate([block[:, :BLK], turned], axis=1)

    pl.semaphore_wait(barrier, n + 1)

    lines = n // 2
    high, low = me // 2, lax.rem(me, 2)
    partner = high * 2 + 1 - low

    def line(k):
        return lax.rem(high + k, lines) * 2

    def at_home(c):
        return table.at[pl.ds(c * blocks, blocks)]

    def across(c):
        return table.at[pl.ds((n + c) * blocks, blocks)]

    first_hop = [
        remote(at_home(me), at_home(me), g_send.at[0, k], g_recv.at[0, k], dist, line(k) + low)
        for k in range(1, lines)
    ]
    for copy in first_hop:
        copy.start()

    def t_part(c):
        return t_ref.at[:, :, pl.ds(pl.multiple_of(c * cols, LANES), cols)]

    tensor = [
        remote(t_part(ahead(k)), trecv.at[me], t_send.at[k], t_recv.at[k], dist, ahead(k)) for k in far_first
    ]
    for copy in tensor:
        copy.start()
    own_t = pltpu.make_async_copy(t_part(me), trecv.at[me], own_sem.at[0])
    own_t.start()

    second_hop, third_hop = [], []
    for k in range(lines):
        if k:
            first_hop[k - 1].wait_recv()
        c = line(lines - k) + low
        second_hop.append(remote(at_home(c), at_home(c), g_send.at[1, k], g_recv.at[1, k], dist, partner))
        second_hop[-1].start()
        third_hop.append(remote(at_home(c), across(c), g_send.at[2, k], g_recv.at[2, k], before, me))
        third_hop[-1].start()

    def turn(s, carry):
        for j in range(chunks):
            tf[j * rows:(j + 1) * rows, :] = t_ref[s, :, j * LANES:(j + 1) * LANES].astype(F32)
        for i in range(rows):
            tt[s, i * chunks:(i + 1) * chunks, :] = tf[pl.ds(i, chunks, stride=rows), :].astype(BF16)
        return carry

    lax.fori_loop(0, slots, turn, 0)

    for k in range(lines):
        second_hop[k].wait_recv()
        c = line(lines - k) + 1 - low
        third_hop.append(remote(at_home(c), across(c), g_send.at[3, k], g_recv.at[3, k], before, me))
        third_hop[-1].start()
    for copy in third_hop:
        copy.wait()
    for copy in first_hop + second_hop:
        copy.wait_send()

    size = atoms * slots
    atom = (dist * n + me) * rows // BLK
    total = n * blocks * groups
    base = dist * n * blocks

    def position(value):
        shift = value - base
        return jnp.minimum(jnp.where(shift < 0, shift + total, shift), 2 * n * blocks - 1)

    step_rows = 8 * chunks
    lane = lax.broadcasted_iota(jnp.int32, (half, LANES), 1)

    def update(s, carry):
        at = (atom * slots + s) * slots
        for r in range(slots):
            src = ids[at + r]
            live = jnp.where(src >= 0, 1.0, 0.0).astype(F32)
            src = jnp.maximum(src, 0)
            virt = table[position(ids[2 * size * slots + at + r])].astype(F32)[:, :BLK] * live
            zero = jnp.zeros((BLK, LANES), F32)
            twice = jnp.concatenate([virt, virt], axis=1)
            weight = jnp.concatenate(
                [jnp.concatenate([twice, zero], axis=1), jnp.concatenate([zero, twice], axis=1)], axis=0
            ).astype(BF16)
            ocat[:, r * BLK:(r + 1) * BLK] = table[position(ids[size * slots + at + r])][:, BLK:]
            for h in range(rows // 8):
                got = jnp.dot(
                    tt[src, h * step_rows:(h + 1) * step_rows, :], weight, preferred_element_type=F32
                ).astype(BF16)
                for x in range(8):
                    i = h * 8 + x
                    for e in range(2):
                        wcat[r * BLK + e * half:r * BLK + (e + 1) * half, i * LANES:(i + 1) * LANES] = got[
                            x * chunks:(x + 1) * chunks, e * LANES:(e + 1) * LANES
                        ]
        occ = ocat[...]
        for h in range(rows // 4):
            both = jnp.dot(occ, wcat[:, h * 4 * LANES:(h + 1) * 4 * LANES], preferred_element_type=F32)
            for x in range(4):
                i = h * 4 + x
                piece = both[:, x * LANES:(x + 1) * LANES]
                tf[i * chunks:(i + 1) * chunks, :] = jnp.where(lane < BLK, piece[:half], piece[half:])
        for q in range(chunks):
            usend[s, q // per, :, (q % per) * LANES:(q % per + 1) * LANES] = tf[
                pl.ds(q, rows, stride=chunks), :
            ].astype(BF16)
        for k in far_first:
            sent(s, k).start()
        return carry

    def sent(s, k):
        return remote(
            usend.at[s, ahead(k)], urecv.at[me, s], u_send.at[s, k], u_recv.at[s, k], dist, ahead(k)
        )

    lax.fori_loop(0, slots, update, 0)
    own_u = pltpu.make_async_copy(usend.at[:, me], urecv.at[me], own_sem.at[1])
    own_u.start()
    own_t.wait()
    for copy in tensor:
        copy.wait()

    first = dist * (n * rows // BLK)
    pairs = 3 * size * slots

    def pick(src, pair, p):
        where = pairs + (first + p * rows // BLK) * slots
        slot = jnp.int32(0)
        live = jnp.int32(0)
        for s in range(slots):
            hit = ids[where + s] == pair
            slot = jnp.where(hit, s, slot)
            live = jnp.where(hit, 1, live)
        return (src[p, slot].astype(F32) * live.astype(F32)).astype(BF16)

    def at_rows(p):
        return pl.ds(pl.multiple_of(p * rows, rows), rows)

    def tensor_pair(pair, carry):
        def gather(p, inner):
            tk[pair, at_rows(p), :] = pick(trecv, pair, p)
            return inner

        return lax.fori_loop(0, n, gather, carry)

    lax.fori_loop(0, NPR, tensor_pair, 0)
    part[...] = jnp.zeros_like(part)

    own_u.wait()
    for s in range(slots):
        for k in range(1, n):
            sent(s, k).wait()

    def one_pair(pair, carry):
        def gather(p, inner):
            uk[at_rows(p), :] = pick(urecv, pair, p)
            return inner

        lax.fori_loop(0, n, gather, 0)

        def block(p, inner):
            at = pl.ds(pl.multiple_of(p * 256, 256), 256)
            part[at, :] += lax.dot_general(
                uk[at, :], tk[pair], (((1,), (1,)), ((), ())), preferred_element_type=F32
            )
            return inner

        lax.fori_loop(0, n * rows // 256, block, 0)
        return carry

    lax.fori_loop(0, NPR, one_pair, 0)

    psend[...] = part[...].astype(BF16)

    def p_part(c):
        return psend.at[pl.ds(pl.multiple_of(c * rows, rows), rows)]

    shares = [
        remote(p_part(ahead(k)), precv.at[k], p_send.at[k], p_recv.at[k], dist, ahead(k)) for k in far_first
    ]
    for copy in shares:
        copy.start()
    result = part[pl.ds(pl.multiple_of(me * rows, rows), rows), :]
    for k, copy in zip(far_first, shares):
        copy.wait()
        result = result + precv[k].astype(F32)
    out_ref[...] = result


def solution(mesh):
    n = mesh.shape["ctr"]
    groups = mesh.shape["dist"]

    def shards(three_centre, occupied_green, virtual_green, pair_index, source_slot, occupied_index, virtual_index):
        rows, slots, width = three_centre.shape
        blocks = occupied_green.shape[0]
        atoms = pair_index.shape[0]
        chunks = width // LANES
        cols = width // n
        tensor = jnp.transpose(three_centre, (1, 0, 2))
        green = jnp.concatenate(
            [virtual_green.reshape(blocks, BLK, BLK), occupied_green.reshape(blocks, BLK, BLK)], axis=2
        )
        ids = jnp.concatenate(
            [x.reshape(-1) for x in (source_slot, occupied_index, virtual_index, pair_index)]
        )
        vmem = pl.BlockSpec(memory_space=pltpu.VMEM)
        dma = pltpu.SemaphoreType.DMA
        return pl.pallas_call(
            functools.partial(kernel, n, groups, atoms),
            out_shape=jax.ShapeDtypeStruct((rows, n * rows), F32),
            in_specs=[pl.BlockSpec(memory_space=pltpu.SMEM), vmem, vmem],
            out_specs=vmem,
            scratch_shapes=[
                pltpu.VMEM((2 * n * blocks, BLK, LANES), BF16),
                pltpu.VMEM((rows * chunks, LANES), F32),
                pltpu.VMEM((slots, rows * chunks, LANES), BF16),
                pltpu.VMEM((slots * BLK, rows * LANES), BF16),
                pltpu.VMEM((BLK, slots * BLK), BF16),
                pltpu.VMEM((slots, n, rows, cols), BF16),
                pltpu.VMEM((n, slots, rows, cols), BF16),
                pltpu.VMEM((n, slots, rows, cols), BF16),
                pltpu.VMEM((n * rows, cols), BF16),
                pltpu.VMEM((NPR, n * rows, cols), BF16),
                pltpu.VMEM((n * rows, n * rows), F32),
                pltpu.VMEM((n * rows, n * rows), BF16),
                pltpu.VMEM((n, rows, n * rows), BF16),
                dma((4, n // 2)),
                dma((4, n // 2)),
                dma((n,)),
                dma((n,)),
                dma((slots, n)),
                dma((slots, n)),
                dma((n,)),
                dma((n,)),
                dma((2,)),
            ],
            compiler_params=pltpu.CompilerParams(
                collective_id=0, has_side_effects=True, vmem_limit_bytes=48 * 2**20
            ),
        )(ids, tensor, green)

    return jax.shard_map(
        shards,
        mesh=mesh,
        in_specs=(
            P(("dist", "ctr"), None, None),
            P(("dist", "ctr"), None),
            P(("dist", "ctr"), None),
            P(),
            P(),
            P(),
            P(),
        ),
        out_specs=P(("dist", "ctr"), None),
        check_vma=False,
    )
```

```python
import functools

import jax
import jax.numpy as jnp
from jax import lax
from jax.experimental import pallas as pl
from jax.experimental.pallas import tpu as pltpu
from jax.sharding import PartitionSpec as P

BLK = 64
NPR = 8
LANES = 128
F32 = jnp.float32
BF16 = jnp.bfloat16


def kernel(n, groups, atoms, ids, t_ref, green_ref, out_ref, table, tf, tt, wcat, ocat, usend, urecv, trecv,
           uk, tk, part, psend, precv, g_send, g_recv, t_send, t_recv, u_send, u_recv, p_send, p_recv, own_sem):
    slots, rows, width = t_ref.shape
    chunks = width // LANES
    blocks = green_ref.shape[0]
    cols = width // n
    per = cols // LANES
    dist = lax.axis_index("dist")
    me = lax.axis_index("ctr")
    before = lax.rem(dist + groups - 1, groups)
    after = lax.rem(dist + 1, groups)

    far_first = sorted(range(1, n), key=lambda k: -min(k, n - k))

    def ahead(k):
        return lax.rem(me + k, n)

    def signal(d, c):
        pl.semaphore_signal(barrier, inc=1, device_id=(d, c), device_id_type=pl.DeviceIdType.MESH)

    def remote(src, dst, send, recv, d, c):
        return pltpu.make_async_remote_copy(
            src_ref=src, dst_ref=dst, send_sem=send, recv_sem=recv, device_id=(d, c),
            device_id_type=pl.DeviceIdType.MESH,
        )

    barrier = pltpu.get_barrier_semaphore()
    for k in range(1, n):
        signal(dist, ahead(k))
    signal(before, me)
    signal(after, me)

    row = lax.broadcasted_iota(jnp.int32, (BLK, BLK), 0)
    col = lax.broadcasted_iota(jnp.int32, (BLK, BLK), 1)
    half = BLK // 2
    wanted = jnp.where(row < half, 2 * row, 2 * (row - half) + 1)
    perm = (wanted == col).astype(BF16)
    mine = me * blocks
    for b in range(blocks):
        block = green_ref[b]
        occ = block[:, BLK:]
        turned = lax.dot_general(perm, occ, (((1,), (1,)), ((), ())), preferred_element_type=F32).astype(BF16)
        turned = lax.dot_general(turned, perm, (((1,), (1,)), ((), ())), preferred_element_type=F32).astype(BF16)
        table[mine + b] = jnp.concatenate([block[:, :BLK], turned], axis=1)

    pl.semaphore_wait(barrier, n + 1)

    lines = n // 2
    high, low = me // 2, lax.rem(me, 2)
    partner = high * 2 + 1 - low

    def line(k):
        return lax.rem(high + k, lines) * 2

    def at_home(c):
        return table.at[pl.ds(c * blocks, blocks)]

    def across(c):
        return table.at[pl.ds((n + c) * blocks, blocks)]

    first_hop = [
        remote(at_home(me), at_home(me), g_send.at[0, k], g_recv.at[0, k], dist, line(k) + low)
        for k in range(1, lines)
    ]
    for copy in first_hop:
        copy.start()

    def t_part(c):
        return t_ref.at[:, :, pl.ds(pl.multiple_of(c * cols, LANES), cols)]

    tensor = [
        remote(t_part(ahead(k)), trecv.at[me], t_send.at[k], t_recv.at[k], dist, ahead(k)) for k in far_first
    ]
    for copy in tensor:
        copy.start()
    own_t = pltpu.make_async_copy(t_part(me), trecv.at[me], own_sem.at[0])
    own_t.start()

    second_hop, third_hop = [], []
    for k in range(lines):
        if k:
            first_hop[k - 1].wait_recv()
        c = line(lines - k) + low
        second_hop.append(remote(at_home(c), at_home(c), g_send.at[1, k], g_recv.at[1, k], dist, partner))
        second_hop[-1].start()
        third_hop.append(remote(at_home(c), across(c), g_send.at[2, k], g_recv.at[2, k], before, me))
        third_hop[-1].start()

    def turn(s, carry):
        for j in range(chunks):
            tf[j * rows:(j + 1) * rows, :] = t_ref[s, :, j * LANES:(j + 1) * LANES].astype(F32)
        for i in range(rows):
            tt[s, i * chunks:(i + 1) * chunks, :] = tf[pl.ds(i, chunks, stride=rows), :].astype(BF16)
        return carry

    lax.fori_loop(0, slots, turn, 0)

    for k in range(lines):
        second_hop[k].wait_recv()
        c = line(lines - k) + 1 - low
        third_hop.append(remote(at_home(c), across(c), g_send.at[3, k], g_recv.at[3, k], before, me))
        third_hop[-1].start()
    for copy in third_hop:
        copy.wait()
    for copy in first_hop + second_hop:
        copy.wait_send()

    size = atoms * slots
    atom = (dist * n + me) * rows // BLK
    total = n * blocks * groups
    base = dist * n * blocks

    def position(value):
        shift = value - base
        return jnp.minimum(jnp.where(shift < 0, shift + total, shift), 2 * n * blocks - 1)

    step_rows = 8 * chunks
    lane = lax.broadcasted_iota(jnp.int32, (half, LANES), 1)

    def update(s, carry):
        at = (atom * slots + s) * slots
        for r in range(slots):
            src = ids[at + r]
            live = jnp.where(src >= 0, 1.0, 0.0).astype(F32)
            src = jnp.maximum(src, 0)
            virt = table[position(ids[2 * size * slots + at + r])].astype(F32)[:, :BLK] * live
            zero = jnp.zeros((BLK, LANES), F32)
            twice = jnp.concatenate([virt, virt], axis=1)
            weight = jnp.concatenate(
                [jnp.concatenate([twice, zero], axis=1), jnp.concatenate([zero, twice], axis=1)], axis=0
            ).astype(BF16)
            ocat[:, r * BLK:(r + 1) * BLK] = table[position(ids[size * slots + at + r])][:, BLK:]
            for h in range(rows // 8):
                got = jnp.dot(
                    tt[src, h * step_rows:(h + 1) * step_rows, :], weight, preferred_element_type=F32
                ).astype(BF16)
                for x in range(8):
                    i = h * 8 + x
                    for e in range(2):
                        wcat[r * BLK + e * half:r * BLK + (e + 1) * half, i * LANES:(i + 1) * LANES] = got[
                            x * chunks:(x + 1) * chunks, e * LANES:(e + 1) * LANES
                        ]
        occ = ocat[...]
        for h in range(rows // 4):
            both = jnp.dot(occ, wcat[:, h * 4 * LANES:(h + 1) * 4 * LANES], preferred_element_type=F32)
            for x in range(4):
                i = h * 4 + x
                piece = both[:, x * LANES:(x + 1) * LANES]
                tf[i * chunks:(i + 1) * chunks, :] = jnp.where(lane < BLK, piece[:half], piece[half:])
        for q in range(chunks):
            usend[s, q // per, :, (q % per) * LANES:(q % per + 1) * LANES] = tf[
                pl.ds(q, rows, stride=chunks), :
            ].astype(BF16)
        for k in far_first:
            sent(s, k).start()
        return carry

    def sent(s, k):
        return remote(
            usend.at[s, ahead(k)], urecv.at[me, s], u_send.at[s, k], u_recv.at[s, k], dist, ahead(k)
        )

    lax.fori_loop(0, slots, update, 0)
    own_u = pltpu.make_async_copy(usend.at[:, me], urecv.at[me], own_sem.at[1])
    own_u.start()
    own_t.wait()
    for copy in tensor:
        copy.wait()

    first = dist * (n * rows // BLK)
    pairs = 3 * size * slots

    def pick(src, pair, p):
        where = pairs + (first + p * rows // BLK) * slots
        slot = jnp.int32(0)
        live = jnp.int32(0)
        for s in range(slots):
            hit = ids[where + s] == pair
            slot = jnp.where(hit, s, slot)
            live = jnp.where(hit, 1, live)
        return (src[p, slot].astype(F32) * live.astype(F32)).astype(BF16)

    def at_rows(p):
        return pl.ds(pl.multiple_of(p * rows, rows), rows)

    def at_cols(pair):
        return pl.ds(pl.multiple_of(pair * cols, LANES), cols)

    def tensor_pair(pair, carry):
        def gather(p, inner):
            tk[at_rows(p), at_cols(pair)] = pick(trecv, pair, p)
            return inner

        return lax.fori_loop(0, n, gather, carry)

    lax.fori_loop(0, NPR, tensor_pair, 0)

    own_u.wait()
    for s in range(slots):
        for k in range(1, n):
            sent(s, k).wait()

    def one_pair(pair, carry):
        def gather(p, inner):
            uk[at_rows(p), at_cols(pair)] = pick(urecv, pair, p)
            return inner

        lax.fori_loop(0, n, gather, 0)

        return carry

    lax.fori_loop(0, NPR, one_pair, 0)

    def block(p, carry):
        at = pl.ds(pl.multiple_of(p * 256, 256), 256)
        total = lax.dot_general(uk[at, :], tk[...], (((1,), (1,)), ((), ())), preferred_element_type=F32)
        part[at, :] = total
        psend[at, :] = total.astype(BF16)
        return carry

    lax.fori_loop(0, n * rows // 256, block, 0)

    def p_part(c):
        return psend.at[pl.ds(pl.multiple_of(c * rows, rows), rows)]

    shares = [
        remote(p_part(ahead(k)), precv.at[k], p_send.at[k], p_recv.at[k], dist, ahead(k)) for k in far_first
    ]
    for copy in shares:
        copy.start()
    result = part[pl.ds(pl.multiple_of(me * rows, rows), rows), :]
    for k, copy in zip(far_first, shares):
        copy.wait()
        result = result + precv[k].astype(F32)
    out_ref[...] = result


def solution(mesh):
    n = mesh.shape["ctr"]
    groups = mesh.shape["dist"]

    def shards(three_centre, occupied_green, virtual_green, pair_index, source_slot, occupied_index, virtual_index):
        rows, slots, width = three_centre.shape
        blocks = occupied_green.shape[0]
        atoms = pair_index.shape[0]
        chunks = width // LANES
        cols = width // n
        tensor = jnp.transpose(three_centre, (1, 0, 2))
        green = jnp.concatenate(
            [virtual_green.reshape(blocks, BLK, BLK), occupied_green.reshape(blocks, BLK, BLK)], axis=2
        )
        ids = jnp.concatenate(
            [x.reshape(-1) for x in (source_slot, occupied_index, virtual_index, pair_index)]
        )
        vmem = pl.BlockSpec(memory_space=pltpu.VMEM)
        dma = pltpu.SemaphoreType.DMA
        return pl.pallas_call(
            functools.partial(kernel, n, groups, atoms),
            out_shape=jax.ShapeDtypeStruct((rows, n * rows), F32),
            in_specs=[pl.BlockSpec(memory_space=pltpu.SMEM), vmem, vmem],
            out_specs=vmem,
            scratch_shapes=[
                pltpu.VMEM((2 * n * blocks, BLK, LANES), BF16),
                pltpu.VMEM((rows * chunks, LANES), F32),
                pltpu.VMEM((slots, rows * chunks, LANES), BF16),
                pltpu.VMEM((slots * BLK, rows * LANES), BF16),
                pltpu.VMEM((BLK, slots * BLK), BF16),
                pltpu.VMEM((slots, n, rows, cols), BF16),
                pltpu.VMEM((n, slots, rows, cols), BF16),
                pltpu.VMEM((n, slots, rows, cols), BF16),
                pltpu.VMEM((n * rows, NPR * cols), BF16),
                pltpu.VMEM((n * rows, NPR * cols), BF16),
                pltpu.VMEM((n * rows, n * rows), F32),
                pltpu.VMEM((n * rows, n * rows), BF16),
                pltpu.VMEM((n, rows, n * rows), BF16),
                dma((4, n // 2)),
                dma((4, n // 2)),
                dma((n,)),
                dma((n,)),
                dma((slots, n)),
                dma((slots, n)),
                dma((n,)),
                dma((n,)),
                dma((2,)),
            ],
            compiler_params=pltpu.CompilerParams(
                collective_id=0, has_side_effects=True, vmem_limit_bytes=48 * 2**20
            ),
        )(ids, tensor, green)

    return jax.shard_map(
        shards,
        mesh=mesh,
        in_specs=(
            P(("dist", "ctr"), None, None),
            P(("dist", "ctr"), None),
            P(("dist", "ctr"), None),
            P(),
            P(),
            P(),
            P(),
        ),
        out_specs=P(("dist", "ctr"), None),
        check_vma=False,
    )
```

```python
import functools

import jax
import jax.numpy as jnp
from jax import lax
from jax.experimental import pallas as pl
from jax.experimental.pallas import tpu as pltpu
from jax.sharding import PartitionSpec as P

BLK = 64
NPR = 8
LANES = 128
F32 = jnp.float32
BF16 = jnp.bfloat16


def kernel(n, groups, atoms, ids, t_ref, green_ref, out_ref, table, tf, tt, wcat, ocat, usend, urecv, trecv,
           uk, tk, part, psend, precv, g_send, g_recv, t_send, t_recv, u_send, u_recv, p_send, p_recv, own_sem):
    slots, rows, width = t_ref.shape
    chunks = width // LANES
    blocks = green_ref.shape[0]
    cols = width // n
    per = cols // LANES
    dist = lax.axis_index("dist")
    me = lax.axis_index("ctr")
    before = lax.rem(dist + groups - 1, groups)
    after = lax.rem(dist + 1, groups)

    far_first = sorted(range(1, n), key=lambda k: -min(k, n - k))

    def ahead(k):
        return lax.rem(me + k, n)

    def signal(d, c):
        pl.semaphore_signal(barrier, inc=1, device_id=(d, c), device_id_type=pl.DeviceIdType.MESH)

    def remote(src, dst, send, recv, d, c):
        return pltpu.make_async_remote_copy(
            src_ref=src, dst_ref=dst, send_sem=send, recv_sem=recv, device_id=(d, c),
            device_id_type=pl.DeviceIdType.MESH,
        )

    barrier = pltpu.get_barrier_semaphore()
    for k in range(1, n):
        signal(dist, ahead(k))
    signal(before, me)
    signal(after, me)

    row = lax.broadcasted_iota(jnp.int32, (BLK, BLK), 0)
    col = lax.broadcasted_iota(jnp.int32, (BLK, BLK), 1)
    half = BLK // 2
    wanted = jnp.where(row < half, 2 * row, 2 * (row - half) + 1)
    perm = (wanted == col).astype(BF16)
    mine = me * blocks
    for b in range(blocks):
        block = green_ref[b]
        occ = block[:, BLK:]
        turned = lax.dot_general(perm, occ, (((1,), (1,)), ((), ())), preferred_element_type=F32).astype(BF16)
        turned = lax.dot_general(turned, perm, (((1,), (1,)), ((), ())), preferred_element_type=F32).astype(BF16)
        table[mine + b] = jnp.concatenate([block[:, :BLK], turned], axis=1)

    pl.semaphore_wait(barrier, n + 1)

    lines = n // 2
    high, low = me // 2, lax.rem(me, 2)
    partner = high * 2 + 1 - low

    def line(k):
        return lax.rem(high + k, lines) * 2

    def at_home(c):
        return table.at[pl.ds(c * blocks, blocks)]

    def across(c):
        return table.at[pl.ds((n + c) * blocks, blocks)]

    first_hop = [
        remote(at_home(me), at_home(me), g_send.at[0, k], g_recv.at[0, k], dist, line(k) + low)
        for k in range(1, lines)
    ]
    for copy in first_hop:
        copy.start()

    def t_part(c):
        return t_ref.at[:, :, pl.ds(pl.multiple_of(c * cols, LANES), cols)]

    tensor = [
        remote(t_part(ahead(k)), trecv.at[me], t_send.at[k], t_recv.at[k], dist, ahead(k)) for k in far_first
    ]
    for copy in tensor:
        copy.start()
    own_t = pltpu.make_async_copy(t_part(me), trecv.at[me], own_sem.at[0])
    own_t.start()

    second_hop, third_hop = [], []
    for k in range(lines):
        if k:
            first_hop[k - 1].wait_recv()
        c = line(lines - k) + low
        second_hop.append(remote(at_home(c), at_home(c), g_send.at[1, k], g_recv.at[1, k], dist, partner))
        second_hop[-1].start()
        third_hop.append(remote(at_home(c), across(c), g_send.at[2, k], g_recv.at[2, k], before, me))
        third_hop[-1].start()

    def turn(s, carry):
        for j in range(chunks):
            tf[j * rows:(j + 1) * rows, :] = t_ref[s, :, j * LANES:(j + 1) * LANES].astype(F32)
        for i in range(rows):
            tt[s, i * chunks:(i + 1) * chunks, :] = tf[pl.ds(i, chunks, stride=rows), :].astype(BF16)
        return carry

    lax.fori_loop(0, slots, turn, 0)

    for k in range(lines):
        second_hop[k].wait_recv()
        c = line(lines - k) + 1 - low
        third_hop.append(remote(at_home(c), across(c), g_send.at[3, k], g_recv.at[3, k], before, me))
        third_hop[-1].start()
    for copy in third_hop:
        copy.wait()
    for copy in first_hop + second_hop:
        copy.wait_send()

    size = atoms * slots
    atom = (dist * n + me) * rows // BLK
    total = n * blocks * groups
    base = dist * n * blocks

    def position(value):
        shift = value - base
        return jnp.minimum(jnp.where(shift < 0, shift + total, shift), 2 * n * blocks - 1)

    step_rows = 8 * chunks
    lane = lax.broadcasted_iota(jnp.int32, (half, LANES), 1)

    def update(s, carry):
        at = (atom * slots + s) * slots
        for r in range(slots):
            src = ids[at + r]
            live = jnp.where(src >= 0, 1.0, 0.0).astype(F32)
            src = jnp.maximum(src, 0)
            virt = table[position(ids[2 * size * slots + at + r])].astype(F32)[:, :BLK] * live
            zero = jnp.zeros((BLK, LANES), F32)
            twice = jnp.concatenate([virt, virt], axis=1)
            weight = jnp.concatenate(
                [jnp.concatenate([twice, zero], axis=1), jnp.concatenate([zero, twice], axis=1)], axis=0
            ).astype(BF16)
            ocat[:, r * BLK:(r + 1) * BLK] = table[position(ids[size * slots + at + r])][:, BLK:]
            for h in range(rows // 8):
                got = jnp.dot(
                    tt[src, h * step_rows:(h + 1) * step_rows, :], weight, preferred_element_type=F32
                ).astype(BF16)
                for x in range(8):
                    i = h * 8 + x
                    for e in range(2):
                        wcat[r * BLK + e * half:r * BLK + (e + 1) * half, i * LANES:(i + 1) * LANES] = got[
                            x * chunks:(x + 1) * chunks, e * LANES:(e + 1) * LANES
                        ]
        occ = ocat[...]
        for h in range(rows // 4):
            both = jnp.dot(occ, wcat[:, h * 4 * LANES:(h + 1) * 4 * LANES], preferred_element_type=F32)
            for x in range(4):
                i = h * 4 + x
                piece = both[:, x * LANES:(x + 1) * LANES]
                tf[i * chunks:(i + 1) * chunks, :] = jnp.where(lane < BLK, piece[:half], piece[half:])
        for q in range(chunks):
            usend[s, q // per, :, (q % per) * LANES:(q % per + 1) * LANES] = tf[
                pl.ds(q, rows, stride=chunks), :
            ].astype(BF16)
        for k in far_first:
            sent(s, k).start()
        return carry

    def sent(s, k):
        return remote(
            usend.at[s, ahead(k)], urecv.at[me, s], u_send.at[s, k], u_recv.at[s, k], dist, ahead(k)
        )

    lax.fori_loop(0, slots, update, 0)
    own_u = pltpu.make_async_copy(usend.at[:, me], urecv.at[me], own_sem.at[1])
    own_u.start()
    own_t.wait()
    for copy in tensor:
        copy.wait()

    first = dist * (n * rows // BLK)
    pairs = 3 * size * slots

    def pick(src, pair, p):
        where = pairs + (first + p * rows // BLK) * slots
        slot = jnp.int32(0)
        live = jnp.int32(0)
        for s in range(slots):
            hit = ids[where + s] == pair
            slot = jnp.where(hit, s, slot)
            live = jnp.where(hit, 1, live)
        return (src[p, slot].astype(F32) * live.astype(F32)).astype(BF16)

    def at_rows(p):
        return pl.ds(pl.multiple_of(p * rows, rows), rows)

    def at_cols(pair):
        return pl.ds(pl.multiple_of(pair * cols, LANES), cols)

    def tensor_pair(pair, carry):
        def gather(p, inner):
            tk[at_rows(p), at_cols(pair)] = pick(trecv, pair, p)
            return inner

        return lax.fori_loop(0, n, gather, carry)

    lax.fori_loop(0, NPR, tensor_pair, 0)

    def updated_pairs(p):
        where = pairs + (first + p * rows // BLK) * slots

        def one_pair(pair, carry):
            chosen = jnp.zeros((rows, cols), F32)
            for s in range(slots):
                hit = jnp.where(ids[where + s] == pair, 1.0, 0.0).astype(F32)
                chosen = chosen + urecv[p, s].astype(F32) * hit
            uk[at_rows(p), at_cols(pair)] = chosen.astype(BF16)
            return carry

        lax.fori_loop(0, NPR, one_pair, 0)

    own_u.wait()
    updated_pairs(me)
    for k in far_first[::-1]:
        for s in range(slots):
            sent(s, k).wait()
        updated_pairs(lax.rem(me - k + n, n))

    def block(p, carry):
        at = pl.ds(pl.multiple_of(p * 256, 256), 256)
        total = lax.dot_general(uk[at, :], tk[...], (((1,), (1,)), ((), ())), preferred_element_type=F32)
        part[at, :] = total
        psend[at, :] = total.astype(BF16)
        return carry

    lax.fori_loop(0, n * rows // 256, block, 0)

    def p_part(c):
        return psend.at[pl.ds(pl.multiple_of(c * rows, rows), rows)]

    shares = [
        remote(p_part(ahead(k)), precv.at[k], p_send.at[k], p_recv.at[k], dist, ahead(k)) for k in far_first
    ]
    for copy in shares:
        copy.start()
    result = part[pl.ds(pl.multiple_of(me * rows, rows), rows), :]
    for k, copy in zip(far_first, shares):
        copy.wait()
        result = result + precv[k].astype(F32)
    out_ref[...] = result


def solution(mesh):
    n = mesh.shape["ctr"]
    groups = mesh.shape["dist"]

    def shards(three_centre, occupied_green, virtual_green, pair_index, source_slot, occupied_index, virtual_index):
        rows, slots, width = three_centre.shape
        blocks = occupied_green.shape[0]
        atoms = pair_index.shape[0]
        chunks = width // LANES
        cols = width // n
        tensor = jnp.transpose(three_centre, (1, 0, 2))
        green = jnp.concatenate(
            [virtual_green.reshape(blocks, BLK, BLK), occupied_green.reshape(blocks, BLK, BLK)], axis=2
        )
        ids = jnp.concatenate(
            [x.reshape(-1) for x in (source_slot, occupied_index, virtual_index, pair_index)]
        )
        vmem = pl.BlockSpec(memory_space=pltpu.VMEM)
        dma = pltpu.SemaphoreType.DMA
        return pl.pallas_call(
            functools.partial(kernel, n, groups, atoms),
            out_shape=jax.ShapeDtypeStruct((rows, n * rows), F32),
            in_specs=[pl.BlockSpec(memory_space=pltpu.SMEM), vmem, vmem],
            out_specs=vmem,
            scratch_shapes=[
                pltpu.VMEM((2 * n * blocks, BLK, LANES), BF16),
                pltpu.VMEM((rows * chunks, LANES), F32),
                pltpu.VMEM((slots, rows * chunks, LANES), BF16),
                pltpu.VMEM((slots * BLK, rows * LANES), BF16),
                pltpu.VMEM((BLK, slots * BLK), BF16),
                pltpu.VMEM((slots, n, rows, cols), BF16),
                pltpu.VMEM((n, slots, rows, cols), BF16),
                pltpu.VMEM((n, slots, rows, cols), BF16),
                pltpu.VMEM((n * rows, NPR * cols), BF16),
                pltpu.VMEM((n * rows, NPR * cols), BF16),
                pltpu.VMEM((n * rows, n * rows), F32),
                pltpu.VMEM((n * rows, n * rows), BF16),
                pltpu.VMEM((n, rows, n * rows), BF16),
                dma((4, n // 2)),
                dma((4, n // 2)),
                dma((n,)),
                dma((n,)),
                dma((slots, n)),
                dma((slots, n)),
                dma((n,)),
                dma((n,)),
                dma((2,)),
            ],
            compiler_params=pltpu.CompilerParams(
                collective_id=0, has_side_effects=True, vmem_limit_bytes=48 * 2**20
            ),
        )(ids, tensor, green)

    return jax.shard_map(
        shards,
        mesh=mesh,
        in_specs=(
            P(("dist", "ctr"), None, None),
            P(("dist", "ctr"), None),
            P(("dist", "ctr"), None),
            P(),
            P(),
            P(),
            P(),
        ),
        out_specs=P(("dist", "ctr"), None),
        check_vma=False,
    )
```

```python
import functools

import jax
import jax.numpy as jnp
from jax import lax
from jax.experimental import pallas as pl
from jax.experimental.pallas import tpu as pltpu
from jax.sharding import PartitionSpec as P

BLK = 64
NPR = 8
LANES = 128
F32 = jnp.float32
BF16 = jnp.bfloat16


def kernel(n, groups, atoms, ids, t_ref, green_ref, out_ref, table, tf, tt, wcat, ocat, usend, urecv, trecv,
           uk, tk, part, psend, precv, g_send, g_recv, t_send, t_recv, u_send, u_recv, p_send, p_recv, own_sem):
    slots, rows, width = t_ref.shape
    chunks = width // LANES
    blocks = green_ref.shape[0] // 2
    cols = width // n
    per = cols // LANES
    dist = lax.axis_index("dist")
    me = lax.axis_index("ctr")
    before = lax.rem(dist + groups - 1, groups)
    after = lax.rem(dist + 1, groups)

    far_first = sorted(range(1, n), key=lambda k: -min(k, n - k))

    def ahead(k):
        return lax.rem(me + k, n)

    def signal(d, c):
        pl.semaphore_signal(barrier, inc=1, device_id=(d, c), device_id_type=pl.DeviceIdType.MESH)

    def remote(src, dst, send, recv, d, c):
        return pltpu.make_async_remote_copy(
            src_ref=src, dst_ref=dst, send_sem=send, recv_sem=recv, device_id=(d, c),
            device_id_type=pl.DeviceIdType.MESH,
        )

    barrier = pltpu.get_barrier_semaphore()
    for k in range(1, n):
        signal(dist, ahead(k))
    signal(before, me)
    signal(after, me)

    row = lax.broadcasted_iota(jnp.int32, (BLK, BLK), 0)
    col = lax.broadcasted_iota(jnp.int32, (BLK, BLK), 1)
    half = BLK // 2
    wanted = jnp.where(row < half, 2 * row, 2 * (row - half) + 1)
    perm = (wanted == col).astype(BF16)
    mine = me * blocks
    for b in range(blocks):
        occ = green_ref[blocks + b]
        turned = lax.dot_general(perm, occ, (((1,), (1,)), ((), ())), preferred_element_type=F32).astype(BF16)
        turned = lax.dot_general(turned, perm, (((1,), (1,)), ((), ())), preferred_element_type=F32).astype(BF16)
        table[mine + b] = jnp.concatenate([green_ref[b], turned], axis=1)

    pl.semaphore_wait(barrier, n + 1)

    lines = n // 2
    high, low = me // 2, lax.rem(me, 2)
    partner = high * 2 + 1 - low

    def line(k):
        return lax.rem(high + k, lines) * 2

    def at_home(c):
        return table.at[pl.ds(c * blocks, blocks)]

    def across(c):
        return table.at[pl.ds((n + c) * blocks, blocks)]

    first_hop = [
        remote(at_home(me), at_home(me), g_send.at[0, k], g_recv.at[0, k], dist, line(k) + low)
        for k in range(1, lines)
    ]
    for copy in first_hop:
        copy.start()

    def t_part(c):
        return t_ref.at[:, :, pl.ds(pl.multiple_of(c * cols, LANES), cols)]

    tensor = [
        remote(t_part(ahead(k)), trecv.at[me], t_send.at[k], t_recv.at[k], dist, ahead(k)) for k in far_first
    ]
    for copy in tensor:
        copy.start()
    own_t = pltpu.make_async_copy(t_part(me), trecv.at[me], own_sem.at[0])
    own_t.start()

    second_hop, third_hop = [], []
    for k in range(lines):
        if k:
            first_hop[k - 1].wait_recv()
        c = line(lines - k) + low
        second_hop.append(remote(at_home(c), at_home(c), g_send.at[1, k], g_recv.at[1, k], dist, partner))
        second_hop[-1].start()
        third_hop.append(remote(at_home(c), across(c), g_send.at[2, k], g_recv.at[2, k], before, me))
        third_hop[-1].start()

    def turn(s, carry):
        for j in range(chunks):
            tf[j * rows:(j + 1) * rows, :] = t_ref[s, :, j * LANES:(j + 1) * LANES].astype(F32)
        for i in range(rows):
            tt[s, i * chunks:(i + 1) * chunks, :] = tf[pl.ds(i, chunks, stride=rows), :].astype(BF16)
        return carry

    lax.fori_loop(0, slots, turn, 0)

    for k in range(lines):
        second_hop[k].wait_recv()
        c = line(lines - k) + 1 - low
        third_hop.append(remote(at_home(c), across(c), g_send.at[3, k], g_recv.at[3, k], before, me))
        third_hop[-1].start()
    for copy in third_hop:
        copy.wait()
    for copy in first_hop + second_hop:
        copy.wait_send()

    size = atoms * slots
    atom = (dist * n + me) * rows // BLK
    total = n * blocks * groups
    base = dist * n * blocks

    def position(value):
        shift = value - base
        return jnp.minimum(jnp.where(shift < 0, shift + total, shift), 2 * n * blocks - 1)

    step_rows = 8 * chunks
    lane = lax.broadcasted_iota(jnp.int32, (half, LANES), 1)

    def update(s, carry):
        at = (atom * slots + s) * slots
        for r in range(slots):
            src = ids[at + r]
            live = jnp.where(src >= 0, 1.0, 0.0).astype(F32)
            src = jnp.maximum(src, 0)
            virt = table[position(ids[2 * size * slots + at + r])].astype(F32)[:, :BLK] * live
            zero = jnp.zeros((BLK, LANES), F32)
            twice = jnp.concatenate([virt, virt], axis=1)
            weight = jnp.concatenate(
                [jnp.concatenate([twice, zero], axis=1), jnp.concatenate([zero, twice], axis=1)], axis=0
            ).astype(BF16)
            ocat[:, r * BLK:(r + 1) * BLK] = table[position(ids[size * slots + at + r])][:, BLK:]
            for h in range(rows // 8):
                got = jnp.dot(
                    tt[src, h * step_rows:(h + 1) * step_rows, :], weight, preferred_element_type=F32
                ).astype(BF16)
                for x in range(8):
                    i = h * 8 + x
                    for e in range(2):
                        wcat[r * BLK + e * half:r * BLK + (e + 1) * half, i * LANES:(i + 1) * LANES] = got[
                            x * chunks:(x + 1) * chunks, e * LANES:(e + 1) * LANES
                        ]
        occ = ocat[...]
        for h in range(rows // 4):
            both = jnp.dot(occ, wcat[:, h * 4 * LANES:(h + 1) * 4 * LANES], preferred_element_type=F32)
            for x in range(4):
                i = h * 4 + x
                piece = both[:, x * LANES:(x + 1) * LANES]
                tf[i * chunks:(i + 1) * chunks, :] = jnp.where(lane < BLK, piece[:half], piece[half:])
        for q in range(chunks):
            usend[s, q // per, :, (q % per) * LANES:(q % per + 1) * LANES] = tf[
                pl.ds(q, rows, stride=chunks), :
            ].astype(BF16)
        for k in far_first:
            sent(s, k).start()
        return carry

    def sent(s, k):
        return remote(
            usend.at[s, ahead(k)], urecv.at[me, s], u_send.at[s, k], u_recv.at[s, k], dist, ahead(k)
        )

    lax.fori_loop(0, slots, update, 0)
    own_u = pltpu.make_async_copy(usend.at[:, me], urecv.at[me], own_sem.at[1])
    own_u.start()
    own_t.wait()
    for copy in tensor:
        copy.wait()

    first = dist * (n * rows // BLK)
    pairs = 3 * size * slots

    def pick(src, pair, p):
        where = pairs + (first + p * rows // BLK) * slots
        slot = jnp.int32(0)
        live = jnp.int32(0)
        for s in range(slots):
            hit = ids[where + s] == pair
            slot = jnp.where(hit, s, slot)
            live = jnp.where(hit, 1, live)
        return (src[p, slot].astype(F32) * live.astype(F32)).astype(BF16)

    def at_rows(p):
        return pl.ds(pl.multiple_of(p * rows, rows), rows)

    def at_cols(pair):
        return pl.ds(pl.multiple_of(pair * cols, LANES), cols)

    def tensor_pair(pair, carry):
        def gather(p, inner):
            tk[at_rows(p), at_cols(pair)] = pick(trecv, pair, p)
            return inner

        return lax.fori_loop(0, n, gather, carry)

    lax.fori_loop(0, NPR, tensor_pair, 0)

    def updated_pairs(p):
        where = pairs + (first + p * rows // BLK) * slots

        def one_pair(pair, carry):
            chosen = jnp.zeros((rows, cols), F32)
            for s in range(slots):
                hit = jnp.where(ids[where + s] == pair, 1.0, 0.0).astype(F32)
                chosen = chosen + urecv[p, s].astype(F32) * hit
            uk[at_rows(p), at_cols(pair)] = chosen.astype(BF16)
            return carry

        lax.fori_loop(0, NPR, one_pair, 0)

    own_u.wait()
    updated_pairs(me)
    for k in far_first[::-1]:
        for s in range(slots):
            sent(s, k).wait()
        updated_pairs(lax.rem(me - k + n, n))

    def block(p, carry):
        at = pl.ds(pl.multiple_of(p * 256, 256), 256)
        total = lax.dot_general(uk[at, :], tk[...], (((1,), (1,)), ((), ())), preferred_element_type=F32)
        part[at, :] = total
        psend[at, :] = total.astype(BF16)
        return carry

    lax.fori_loop(0, n * rows // 256, block, 0)

    def p_part(c):
        return psend.at[pl.ds(pl.multiple_of(c * rows, rows), rows)]

    shares = [
        remote(p_part(ahead(k)), precv.at[k], p_send.at[k], p_recv.at[k], dist, ahead(k)) for k in far_first
    ]
    for copy in shares:
        copy.start()
    result = part[pl.ds(pl.multiple_of(me * rows, rows), rows), :]
    for k, copy in zip(far_first, shares):
        copy.wait()
        result = result + precv[k].astype(F32)
    out_ref[...] = result


def solution(mesh):
    n = mesh.shape["ctr"]
    groups = mesh.shape["dist"]

    def shards(three_centre, occupied_green, virtual_green, pair_index, source_slot, occupied_index, virtual_index):
        rows, slots, width = three_centre.shape
        blocks = occupied_green.shape[0]
        atoms = pair_index.shape[0]
        chunks = width // LANES
        cols = width // n
        tensor = jnp.transpose(three_centre, (1, 0, 2))
        green = jnp.concatenate([virtual_green, occupied_green], axis=0).reshape(2 * blocks, BLK, BLK)
        ids = jnp.concatenate(
            [x.reshape(-1) for x in (source_slot, occupied_index, virtual_index, pair_index)]
        )
        vmem = pl.BlockSpec(memory_space=pltpu.VMEM)
        dma = pltpu.SemaphoreType.DMA
        return pl.pallas_call(
            functools.partial(kernel, n, groups, atoms),
            out_shape=jax.ShapeDtypeStruct((rows, n * rows), F32),
            in_specs=[pl.BlockSpec(memory_space=pltpu.SMEM), vmem, vmem],
            out_specs=vmem,
            scratch_shapes=[
                pltpu.VMEM((2 * n * blocks, BLK, LANES), BF16),
                pltpu.VMEM((rows * chunks, LANES), F32),
                pltpu.VMEM((slots, rows * chunks, LANES), BF16),
                pltpu.VMEM((slots * BLK, rows * LANES), BF16),
                pltpu.VMEM((BLK, slots * BLK), BF16),
                pltpu.VMEM((slots, n, rows, cols), BF16),
                pltpu.VMEM((n, slots, rows, cols), BF16),
                pltpu.VMEM((n, slots, rows, cols), BF16),
                pltpu.VMEM((n * rows, NPR * cols), BF16),
                pltpu.VMEM((n * rows, NPR * cols), BF16),
                pltpu.VMEM((n * rows, n * rows), F32),
                pltpu.VMEM((n * rows, n * rows), BF16),
                pltpu.VMEM((n, rows, n * rows), BF16),
                dma((4, n // 2)),
                dma((4, n // 2)),
                dma((n,)),
                dma((n,)),
                dma((slots, n)),
                dma((slots, n)),
                dma((n,)),
                dma((n,)),
                dma((2,)),
            ],
            compiler_params=pltpu.CompilerParams(
                collective_id=0, has_side_effects=True, vmem_limit_bytes=48 * 2**20
            ),
        )(ids, tensor, green)

    return jax.shard_map(
        shards,
        mesh=mesh,
        in_specs=(
            P(("dist", "ctr"), None, None),
            P(("dist", "ctr"), None),
            P(("dist", "ctr"), None),
            P(),
            P(),
            P(),
            P(),
        ),
        out_specs=P(("dist", "ctr"), None),
        check_vma=False,
    )
```
